32 devices in a mesh: parts: 2 (over y), seq: 4 (over z), mp: 2 (over x), batch: 2 (over core).
Axes of the slice: x: 2, y: 2, z: 4, core: 2. Of those that a mesh axis runs over, the one named last changes fastest.
Arguments:
- hidden_acts: bfloat16 [4, 4096, 14336], P(('parts', 'batch'), 'seq', 'mp'), parts along dimension 0, may hold values from -6 to 6
- out_cotangent: bfloat16 [4, 4096, 4096], P(('parts', 'batch'), 'seq', 'mp'), parts along dimension 0, may hold values from -6 to 6
- in_projection: bfloat16 [14336, 64], P('mp'), may hold values from -0.046875 to 0.046875
- out_projection: bfloat16 [4096, 64], P('mp'), may hold values from -0.09375 to 0.09375
- step_lengths: int32 [4, 128], P(('parts', 'batch')), parts along dimension 0, may hold values from 1 to 2048, 4096 in all within a row
- query_grads: bfloat16 [256, 4096], P('seq', 'mp'), may hold values from -0.01171875 to 0.01171875
- query_trace: int32 [256], replicated, may hold values from 0 to 1
Outputs:
- scores: float32 [4, 128, 256], P(('parts', 'batch'), 'seq'), parts along dimension 0
The draws below stay inside these ranges and needn't reach their ends.
There are 2 independent parts, one for each index of `parts`. The reference program is written for one: setup_inputs(seed, part) draws one part's arguments, and reference() takes and returns one part's arrays. A program takes and returns all parts, laid end to end along the dimension named above; an argument that names none is the same for every part. Nothing has to cross between parts.
Inputs may be any that keep to these rules, and one draw needn't show every extreme that they name: `step_lengths`: the 128 lengths of each trace add up to 4096, and the longest is 2048.
All inputs are finite; a program needn't handle non-finite values.
Results may differ from the reference program's by a relative error of at most 0.0051.
Values may be sent and summed in bfloat16 or wider, within the bound.
A program may use at most 64 MiB of HBM per device.

```python
import math
import jax
import jax.numpy as jnp
import numpy as np
from jax import lax

D = 4096
FF = 14336
RANK = 64
TRACES = 2
LEN = 4096
STEPS = 128
QUERIES = 256
MOST = 2048
FEAT = 4096


def touch_ends(values, stream_key, low, largest):
    dims = values.shape
    index_at = [jax.random.randint(jax.random.fold_in(stream_key, axis), (), 0, dims[axis]) for axis in range(len(dims))]
    values = values.at[tuple(index_at)].set(low)
    longest = dims.index(max(dims))
    index_at[longest] = (index_at[longest] + 1) % dims[longest]
    return values.at[tuple(index_at)].set(largest)


def steps_of(rng, shape, pieces, smallest, high):
    level, own = 1.0, jax.random.fold_in(rng, 6)
    for axis_at, shards_of in pieces:
        draws = jnp.exp(jax.random.uniform(jax.random.fold_in(own, axis_at), (shards_of,), jnp.float32, smallest / len(pieces), high / len(pieces)))
        level = level * jnp.repeat(draws, shape[axis_at] // shards_of).reshape([-1 if axis == axis_at else 1 for axis in range(len(shape))])
    return level


def profile(number_of, total, most, skew):
    portions = [(1 << 20) // math.isqrt(standing ** skew) + 1 for standing in range(2, number_of + 1)]
    surplus, given = total - most - (number_of - 1), [1] * (number_of - 1)
    while surplus > 0:
        free = [i for i in range(number_of - 1) if given[i] < most]
        pool, remaining = sum([portions[i] for i in free]), surplus
        for i in free:
            extra = min(most - given[i], max(1, remaining * portions[i] // pool), surplus)
            given[i] = given[i] + extra
            surplus = surplus - extra
    return np.array([most] + given)


def ragged_sizes(rng, amount, total, limit, skew):
    if amount == 2:
        one = jax.random.randint(rng, (), max(1, total - limit), min(limit, total - 1) + 1)
        return jnp.stack([one, total - one])
    sizes = jnp.asarray(profile(amount, total, limit, skew), jnp.int32)
    twos = (amount - 1) // 2
    giver, receiver = sizes[1:1 + 2 * twos:2], sizes[2:2 + 2 * twos:2]
    room = jnp.minimum(giver - 1, limit - receiver)
    shifted = jax.random.randint(jax.random.fold_in(rng, 1), (twos,), 0, 1 << 20) % (room + 1)
    sizes = sizes.at[1:1 + 2 * twos:2].set(giver - shifted).at[2:2 + 2 * twos:2].set(receiver + shifted)
    return sizes[jax.random.permutation(jax.random.fold_in(rng, 2), amount)]


def noise(stream_key, dims, width, reach, shards=(), held_as=jnp.bfloat16):
    array = jax.random.normal(stream_key, dims, jnp.float32) * width
    if len(shards) > 0:
        array = steps_of(stream_key, dims, shards, -0.22, 0.18) * array
    return jnp.clip(array, min=-reach, max=reach).astype(held_as)


def setup_inputs(seed: int = 0, part: int = 0) -> dict:
    arg_keys = jax.random.split(jax.random.key(seed), 8)
    part_splits = jax.random.split(jax.random.fold_in(arg_keys[7], part), 8)
    hidden_acts = noise(part_splits[0], (TRACES, LEN, FF), 1.0, 6.0, ((0, 2), (1, 4), (2, 2)))
    out_cotangent = noise(part_splits[1], (TRACES, LEN, D), 1.0, 6.0, ((0, 2), (1, 4), (2, 2)))
    in_projection = noise(arg_keys[2], (FF, RANK), FF ** -0.5, 0.046875, ((0, 2),))
    out_projection = noise(arg_keys[3], (D, RANK), D ** -0.5, 0.09375, ((0, 2),))
    step_lengths = jax.vmap(lambda own: ragged_sizes(own, STEPS, LEN, MOST, 2))(jax.random.split(part_splits[4], TRACES)).reshape((TRACES, STEPS)).astype(jnp.int32)
    query_grads = noise(arg_keys[5], (QUERIES, FEAT), 0.002, 0.01171875, ((0, 4), (1, 2)))
    query_trace = touch_ends(jax.random.randint(arg_keys[6], (QUERIES,), 0, TRACES), jax.random.fold_in(arg_keys[6], 1), 0, TRACES - 1).astype(jnp.int32)
    return {"hidden_acts": hidden_acts, "out_cotangent": out_cotangent, "in_projection": in_projection, "out_projection": out_projection, "step_lengths": step_lengths, "query_grads": query_grads, "query_trace": query_trace}


def reference(hidden_acts, out_cotangent, in_projection, out_projection, step_lengths, query_grads, query_trace):
    def one_trace(inputs):
        activations, cotangent, lengths, trace_index = inputs
        in_factors = jnp.dot(activations, in_projection, preferred_element_type=jnp.float32).astype(jnp.bfloat16).astype(jnp.float32)
        out_factors = jnp.dot(cotangent, out_projection, preferred_element_type=jnp.float32).astype(jnp.bfloat16).astype(jnp.float32)
        step_ends = jnp.cumsum(lengths, dtype=jnp.int32)
        step_starts = step_ends - lengths
        positions = jnp.arange(LEN, dtype=jnp.int32)
        member = ((positions[None, :] >= step_starts[:, None]) & (positions[None, :] < step_ends[:, None])).astype(jnp.float32)
        outer = (out_factors[:, :, None] * in_factors[:, None, :]).reshape(LEN, RANK * RANK)
        step_grads = jnp.dot(member, outer, precision=lax.Precision.HIGHEST, preferred_element_type=jnp.float32)
        step_low = step_grads.astype(jnp.bfloat16)
        raw_scores = lax.dot_general(step_low, query_grads, (((1,), (1,)), ((), ())), preferred_element_type=jnp.float32)
        keep = query_trace != trace_index
        return jnp.where(keep[None, :], raw_scores, jnp.zeros((), jnp.float32))

    trace_ids = jnp.arange(TRACES, dtype=jnp.int32)
    return lax.map(one_trace, (hidden_acts, out_cotangent, step_lengths, trace_ids))
```

```python
import functools

import jax
import jax.numpy as jnp
from jax import lax
from jax.experimental import pallas as pl
from jax.experimental.pallas import tpu as pltpu
from jax.sharding import PartitionSpec as P

MESH = pl.DeviceIdType.MESH
CHUNK = 256
GROUP = 4


def nt(left, right):
    return lax.dot_general(
        left, right, (((1,), (1,)), ((), ())), preferred_element_type=jnp.float32
    )


def kernel(
    nseq, nmp, nb,
    hid_hbm, cot_hbm, win_hbm, wout_hbm, len_ref, q_hbm,
    out_ref,
    hid, cot, win, wout, qbuf, inbuf, outown, outrecv, gacc, sbuf, srecv,
    hid_sem, cot_sem, w_sem, qloc_sem,
    in_ssem, in_rsem, out_ssem, out_rsem, q_ssem, q_rsem, qb_ssem, qb_rsem, s_ssem, s_rsem,
):
    tokens = hid.shape[0]
    rank = win.shape[1]
    share = rank // nmp
    steps = len_ref.shape[1]
    chunks = tokens // CHUNK
    mine = steps // nseq
    z = lax.axis_index("seq")
    x = lax.axis_index("mp")
    b = lax.axis_index("batch")

    w_copies = [
        pltpu.make_async_copy(wout_hbm, wout, w_sem.at[0]),
        pltpu.make_async_copy(win_hbm, win, w_sem.at[1]),
    ]
    rows = lambda c: pl.ds(c * CHUNK, CHUNK)
    cot_copies = [
        pltpu.make_async_copy(cot_hbm.at[0, rows(c)], cot.at[rows(c)], cot_sem.at[c])
        for c in range(chunks)
    ]
    hid_copies = [
        pltpu.make_async_copy(hid_hbm.at[0, rows(c)], hid.at[rows(c)], hid_sem.at[c])
        for c in range(chunks)
    ]
    q_local = pltpu.make_async_copy(q_hbm, qbuf.at[z], qloc_sem)
    w_copies[0].start()
    for copy in cot_copies:
        copy.start()
    w_copies[1].start()
    hid_copies[0].start()
    q_local.start()
    for copy in hid_copies[1:]:
        copy.start()

    barrier = pltpu.get_barrier_semaphore()
    total = nseq * nmp
    flat = z * nmp + x

    def greet(d, carry):
        peer = lax.rem(flat + d, total)
        pl.semaphore_signal(
            barrier, inc=1, device_id={"seq": peer // nmp, "mp": lax.rem(peer, nmp)},
            device_id_type=MESH,
        )
        return carry

    lax.fori_loop(1, total, greet, 0)
    for d in range(1, nb):
        pl.semaphore_signal(
            barrier, inc=1, device_id={"batch": lax.rem(b + d, nb)}, device_id_type=MESH
        )
    pl.semaphore_wait(barrier, total - 1 + nb - 1)

    def q_copy(owner, peer):
        return pltpu.make_async_remote_copy(
            src_ref=q_hbm.at[b], dst_ref=qbuf.at[owner, b],
            send_sem=q_ssem.at[peer], recv_sem=q_rsem.at[owner],
            device_id={"seq": peer}, device_id_type=MESH,
        )

    def qb_copy(owner, core, peer):
        return pltpu.make_async_remote_copy(
            src_ref=qbuf.at[owner, core], dst_ref=qbuf.at[owner, core],
            send_sem=qb_ssem.at[owner, peer], recv_sem=qb_rsem.at[owner, core],
            device_id={"batch": peer}, device_id_type=MESH,
        )

    others_z = [lax.rem(z + d, nseq) for d in range(1, nseq)]
    others_x = [lax.rem(x + d, nmp) for d in range(1, nmp)]
    others_b = [lax.rem(b + d, nb) for d in range(1, nb)]
    for peer in others_z:
        q_copy(z, peer).start()

    def out_copy(owner, peer, c):
        return pltpu.make_async_remote_copy(
            src_ref=outown.at[c, peer], dst_ref=outrecv.at[c, owner],
            send_sem=out_ssem.at[c, peer], recv_sem=out_rsem.at[c, owner],
            device_id={"mp": peer}, device_id_type=MESH,
        )

    def in_copy(owner, peer, c):
        return pltpu.make_async_remote_copy(
            src_ref=inbuf.at[c, x], dst_ref=inbuf.at[c, owner],
            send_sem=in_ssem.at[c, peer], recv_sem=in_rsem.at[c, owner],
            device_id={"mp": peer}, device_id_type=MESH,
        )

    w_copies[0].wait()
    for c in range(chunks):
        cot_copies[c].wait()
        part = jnp.dot(cot[rows(c), :], wout[...], preferred_element_type=jnp.float32)
        outown[c] = part.T.reshape(nmp, share, CHUNK)
        for peer in others_x:
            out_copy(x, peer, c).start()
        outrecv[c, x] = outown[c, x]

    lengths = len_ref[...].astype(jnp.float32)
    row = lax.broadcasted_iota(jnp.int32, (steps, steps), 0)
    col = lax.broadcasted_iota(jnp.int32, (steps, steps), 1)
    spread = jnp.broadcast_to(lengths, (steps, steps))
    ends = jnp.sum(jnp.where(col <= row, spread, 0.0), axis=1, keepdims=True).astype(jnp.int32)
    starts = jnp.sum(jnp.where(col < row, spread, 0.0), axis=1, keepdims=True).astype(jnp.int32)

    def project(c):
        if c == 0:
            w_copies[1].wait()
        hid_copies[c].wait()
        part = jnp.dot(hid[rows(c), :], win[...], preferred_element_type=jnp.float32)
        inbuf[c, x] = part.T
        for peer in others_x:
            in_copy(x, peer, c).start()

    def gradients(c):
        for peer in others_x:
            out_copy(peer, peer, c).wait_recv()
            in_copy(peer, peer, c).wait_recv()
        out_total = outrecv[c, 0]
        in_total = inbuf[c, 0]
        for m in range(1, nmp):
            out_total = out_total + outrecv[c, m]
            in_total = in_total + inbuf[c, m]
        out_low = out_total.astype(jnp.bfloat16).astype(jnp.float32)
        in_low = in_total.astype(jnp.bfloat16)
        pos = (
            lax.broadcasted_iota(jnp.int32, (steps, CHUNK), 1) + (z * tokens + c * CHUNK)
        )
        member = jnp.where((pos >= starts) & (pos < ends), 1.0, 0.0).astype(jnp.bfloat16)
        member = member.reshape(steps // 16, 16, CHUNK)
        zero = jnp.zeros((rank, CHUNK), jnp.bfloat16)
        right = jnp.concatenate(
            [
                jnp.concatenate([in_low if i == k else zero for i in range(GROUP)], axis=1)
                for k in range(GROUP)
            ],
            axis=0,
        )
        width = GROUP * rank
        for g in range(share // GROUP):
            left = []
            for j in range(g * GROUP, (g + 1) * GROUP):
                line = jnp.broadcast_to(out_low[j:j + 1, :], (16, CHUNK)).astype(jnp.bfloat16)
                left.append((member * line[None]).reshape(steps, CHUNK))
            term = nt(jnp.concatenate(left, axis=1), right)
            at = pl.ds(g * width, width)
            if c == 0:
                gacc[:, at] = term
            else:
                gacc[:, at] += term

    project(0)
    for c in range(1, chunks):
        project(c)
        gradients(c - 1)

    for owner in others_z:
        q_copy(owner, owner).wait_recv()
        for peer in others_b:
            qb_copy(owner, b, peer).start()
    gradients(chunks - 1)
    low = gacc[...].astype(jnp.bfloat16)
    q_local.wait()
    for owner in others_z:
        for core in others_b:
            qb_copy(owner, core, core).wait_recv()
    queries = qbuf[...].reshape(nseq * nb * qbuf.shape[2], qbuf.shape[3])
    part = nt(low, queries).astype(jnp.bfloat16)
    sbuf[...] = part.reshape(nseq, mine, part.shape[1])
    srecv[flat] = sbuf[z]

    def s_copy(owner, peer):
        return pltpu.make_async_remote_copy(
            src_ref=sbuf.at[peer // nmp], dst_ref=srecv.at[owner],
            send_sem=s_ssem.at[peer], recv_sem=s_rsem.at[owner],
            device_id={"seq": peer // nmp, "mp": lax.rem(peer, nmp)}, device_id_type=MESH,
        )

    def s_start(d, carry):
        s_copy(flat, lax.rem(flat + d, total)).start()
        return carry

    def s_wait(d, carry):
        peer = lax.rem(flat + d, total)
        s_copy(peer, peer).wait_recv()
        return carry

    def s_done(d, carry):
        s_copy(flat, lax.rem(flat + d, total)).wait_send()
        return carry

    lax.fori_loop(1, total, s_start, 0)
    for peer in others_z:
        q_copy(z, peer).wait_send()
    for owner in others_z:
        for peer in others_b:
            qb_copy(owner, b, peer).wait_send()
    for c in range(chunks):
        for peer in others_x:
            out_copy(x, peer, c).wait_send()
            in_copy(x, peer, c).wait_send()
    lax.fori_loop(1, total, s_wait, 0)
    out_ref[...] = lax.fori_loop(
        1, total, lambda i, acc: acc + srecv[i].astype(jnp.float32),
        srecv[0].astype(jnp.float32),
    )
    lax.fori_loop(1, total, s_done, 0)


def per_device(
    nseq, nmp, nb,
    hidden_acts, out_cotangent, in_projection, out_projection, step_lengths, query_grads, query_trace,
):
    tokens, units = hidden_acts.shape[1:]
    features = out_cotangent.shape[2]
    rank = in_projection.shape[1]
    share = rank // nmp
    steps = step_lengths.shape[1]
    local, entries = query_grads.shape
    queries = local * nseq
    chunks = tokens // CHUNK
    mine = steps // nseq
    total = nseq * nmp
    any_spec = pl.BlockSpec(memory_space=pl.ANY)
    vmem_spec = pl.BlockSpec(memory_space=pltpu.VMEM)
    dma = pltpu.SemaphoreType.DMA
    totals = pl.pallas_call(
        functools.partial(kernel, nseq, nmp, nb),
        out_shape=jax.ShapeDtypeStruct((mine, queries), jnp.float32),
        in_specs=[any_spec, any_spec, any_spec, any_spec, vmem_spec, any_spec],
        out_specs=vmem_spec,
        scratch_shapes=[
            pltpu.VMEM((tokens, units), jnp.bfloat16),
            pltpu.VMEM((tokens, features), jnp.bfloat16),
            pltpu.VMEM((units, rank), jnp.bfloat16),
            pltpu.VMEM((features, rank), jnp.bfloat16),
            pltpu.VMEM((nseq, nb, local // nb, entries), jnp.bfloat16),
            pltpu.VMEM((chunks, nmp, rank, CHUNK), jnp.float32),
            pltpu.VMEM((chunks, nmp, share, CHUNK), jnp.float32),
            pltpu.VMEM((chunks, nmp, share, CHUNK), jnp.float32),
            pltpu.VMEM((steps, share * rank), jnp.float32),
            pltpu.VMEM((nseq, mine, queries), jnp.bfloat16),
            pltpu.VMEM((total, mine, queries), jnp.bfloat16),
            dma((chunks,)), dma((chunks,)), dma((2,)), dma,
            dma((chunks, nmp)), dma((chunks, nmp)), dma((chunks, nmp)), dma((chunks, nmp)),
            dma((nseq,)), dma((nseq,)), dma((nseq, nb)), dma((nseq, nb)),
            dma((total,)), dma((total,)),
        ],
        compiler_params=pltpu.CompilerParams(
            collective_id=0, has_side_effects=True, vmem_limit_bytes=56 * 1024 * 1024
        ),
        cost_estimate=pl.CostEstimate(
            flops=2 * tokens * (units + features) * rank + 2 * steps * share * tokens * rank,
            bytes_accessed=2 * tokens * (units + features), transcendentals=0,
        ),
        name="influence",
    )(
        hidden_acts, out_cotangent, in_projection, out_projection, step_lengths,
        query_grads.reshape(nb, local // nb, entries),
    )
    keep = query_trace[None, :] != lax.axis_index("batch")
    return jnp.where(keep, totals, jnp.zeros((), jnp.float32))[None]


def solution(mesh):
    return jax.shard_map(
        functools.partial(per_device, mesh.shape["seq"], mesh.shape["mp"], mesh.shape["batch"]),
        mesh=mesh,
        in_specs=(
            P(("parts", "batch"), "seq", "mp"),
            P(("parts", "batch"), "seq", "mp"),
            P("mp", None),
            P("mp", None),
            P(("parts", "batch"), None),
            P("seq", "mp"),
            P(),
        ),
        out_specs=P(("parts", "batch"), "seq", None),
        check_vma=False,
    )
```

```python
import functools

import jax
import jax.numpy as jnp
from jax import lax
from jax.experimental import pallas as pl
from jax.experimental.pallas import tpu as pltpu
from jax.sharding import PartitionSpec as P

MESH = pl.DeviceIdType.MESH
CHUNK = 256
GROUP = 4
DEPTH = 1
LAG = 2


def nt(left, right):
    return lax.dot_general(
        left, right, (((1,), (1,)), ((), ())), preferred_element_type=jnp.float32
    )


def kernel(
    nseq, nmp, nb,
    hid_hbm, cot_hbm, win_hbm, wout_hbm, len_ref, q_hbm,
    out_ref,
    hid, cot, win, wout, qbuf, inbuf, outown, outrecv, lhs, gacc, sbuf, srecv,
    hid_sem, cot_sem, w_sem, qloc_sem,
    in_ssem, in_rsem, out_ssem, out_rsem, q_ssem, q_rsem, qb_ssem, qb_rsem, s_ssem, s_rsem,
):
    tokens = hid.shape[0]
    rank = win.shape[0]
    share = rank // nmp
    steps = len_ref.shape[1]
    chunks = tokens // CHUNK
    mine = steps // nseq
    z = lax.axis_index("seq")
    x = lax.axis_index("mp")
    b = lax.axis_index("batch")

    w_copies = [
        pltpu.make_async_copy(wout_hbm, wout, w_sem.at[0]),
        pltpu.make_async_copy(win_hbm, win, w_sem.at[1]),
    ]
    rows = lambda c: pl.ds(pl.multiple_of(c * CHUNK, CHUNK), CHUNK)

    def cot_copy(c):
        return pltpu.make_async_copy(cot_hbm.at[0, rows(c)], cot.at[rows(c)], cot_sem.at[c])

    def hid_copy(c):
        return pltpu.make_async_copy(hid_hbm.at[0, rows(c)], hid.at[rows(c)], hid_sem.at[c])

    q_local = pltpu.make_async_copy(q_hbm, qbuf.at[z], qloc_sem)
    w_copies[0].start()
    for c in range(chunks):
        cot_copy(c).start()
    w_copies[1].start()
    for c in range(min(DEPTH, chunks)):
        hid_copy(c).start()

    barrier = pltpu.get_barrier_semaphore()
    total = nseq * nmp
    flat = z * nmp + x

    def greet(d, carry):
        peer = lax.rem(flat + d, total)
        pl.semaphore_signal(
            barrier, inc=1, device_id={"seq": peer // nmp, "mp": lax.rem(peer, nmp)},
            device_id_type=MESH,
        )
        return carry

    lax.fori_loop(1, total, greet, 0)
    for d in range(1, nb):
        pl.semaphore_signal(
            barrier, inc=1, device_id={"batch": lax.rem(b + d, nb)}, device_id_type=MESH
        )
    pl.semaphore_wait(barrier, total - 1 + nb - 1)

    def q_copy(owner, peer):
        return pltpu.make_async_remote_copy(
            src_ref=q_hbm.at[b], dst_ref=qbuf.at[owner, b],
            send_sem=q_ssem.at[peer], recv_sem=q_rsem.at[owner],
            device_id={"seq": peer}, device_id_type=MESH,
        )

    def qb_copy(owner, core, peer):
        return pltpu.make_async_remote_copy(
            src_ref=qbuf.at[owner, core], dst_ref=qbuf.at[owner, core],
            send_sem=qb_ssem.at[owner, peer], recv_sem=qb_rsem.at[owner, core],
            device_id={"batch": peer}, device_id_type=MESH,
        )

    others_z = [lax.rem(z + d, nseq) for d in range(1, nseq)]
    others_x = [lax.rem(x + d, nmp) for d in range(1, nmp)]
    others_b = [lax.rem(b + d, nb) for d in range(1, nb)]
    for peer in others_z:
        q_copy(z, peer).start()

    def out_copy(owner, peer, c):
        return pltpu.make_async_remote_copy(
            src_ref=outown.at[c, peer], dst_ref=outrecv.at[c, owner],
            send_sem=out_ssem.at[c, peer], recv_sem=out_rsem.at[c, owner],
            device_id={"mp": peer}, device_id_type=MESH,
        )

    def in_copy(owner, peer, c):
        return pltpu.make_async_remote_copy(
            src_ref=inbuf.at[c, x], dst_ref=inbuf.at[c, owner],
            send_sem=in_ssem.at[c, peer], recv_sem=in_rsem.at[c, owner],
            device_id={"mp": peer}, device_id_type=MESH,
        )

    w_copies[0].wait()

    def features_step(c, carry):
        cot_copy(c).wait()
        part = nt(cot[rows(c), :], wout[...])
        outown[c] = part.T.reshape(nmp, share, CHUNK)
        for peer in others_x:
            out_copy(x, peer, c).start()
        outrecv[c, x] = outown[c, x]
        return carry

    lax.fori_loop(0, chunks, features_step, 0)

    lengths = len_ref[...].astype(jnp.float32)
    row = lax.broadcasted_iota(jnp.int32, (steps, steps), 0)
    col = lax.broadcasted_iota(jnp.int32, (steps, steps), 1)
    spread = jnp.broadcast_to(lengths, (steps, steps))
    ends = jnp.sum(jnp.where(col <= row, spread, 0.0), axis=1, keepdims=True).astype(jnp.int32)
    starts = jnp.sum(jnp.where(col < row, spread, 0.0), axis=1, keepdims=True).astype(jnp.int32)

    def project(c):
        hid_copy(c).wait()

        @pl.when(c < chunks - DEPTH)
        def _():
            hid_copy(c + DEPTH).start()

        part = nt(hid[rows(c), :], win[...])
        inbuf[c, x] = part.T
        for peer in others_x:
            in_copy(x, peer, c).start()

    def gradients(c):
        for peer in others_x:
            out_copy(peer, peer, c).wait_recv()
            in_copy(peer, peer, c).wait_recv()
        out_total = outrecv[c, 0]
        in_total = inbuf[c, 0]
        for m in range(1, nmp):
            out_total = out_total + outrecv[c, m]
            in_total = in_total + inbuf[c, m]
        out_low = out_total.astype(jnp.bfloat16).astype(jnp.float32)
        in_low = in_total.astype(jnp.bfloat16)
        pos = (
            lax.broadcasted_iota(jnp.int32, (steps, CHUNK), 1) + (z * tokens + c * CHUNK)
        )
        member = jnp.where((pos >= starts) & (pos < ends), 1.0, 0.0).astype(jnp.bfloat16)
        member = member.reshape(steps // 16, 16, CHUNK)
        zero = jnp.zeros((rank, CHUNK), jnp.bfloat16)
        right = jnp.concatenate(
            [
                jnp.concatenate([in_low if i == k else zero for i in range(GROUP)], axis=1)
                for k in range(GROUP)
            ],
            axis=0,
        )
        for j in range(share):
            line = jnp.broadcast_to(out_low[j:j + 1, :], (16, CHUNK)).astype(jnp.bfloat16)
            lhs[
                pl.ds(j // GROUP * steps, steps), pl.ds(j % GROUP * CHUNK, CHUNK)
            ] = (member * line[None]).reshape(steps, CHUNK)
        gacc[...] += nt(lhs[...], right)

    gacc[...] = jnp.zeros_like(gacc)
    w_copies[1].wait()

    def hidden_step(c, carry):
        @pl.when(c < chunks)
        def _():
            project(c)

        @pl.when(c >= LAG)
        def _():
            gradients(c - LAG)

        return carry

    q_local.start()
    lax.fori_loop(0, chunks + LAG, hidden_step, 0)

    for owner in others_z:
        q_copy(owner, owner).wait_recv()
        for peer in others_b:
            qb_copy(owner, b, peer).start()
    low = jnp.concatenate(
        [gacc[pl.ds(g * steps, steps), :].astype(jnp.bfloat16) for g in range(share // GROUP)],
        axis=1,
    )
    q_local.wait()
    for owner in others_z:
        for core in others_b:
            qb_copy(owner, core, core).wait_recv()
    queries = qbuf[...].reshape(nseq * nb * qbuf.shape[2], qbuf.shape[3])
    part = nt(low, queries).astype(jnp.bfloat16)
    sbuf[...] = part.reshape(nseq, mine, part.shape[1])
    srecv[flat] = sbuf[z]

    def s_copy(owner, peer):
        return pltpu.make_async_remote_copy(
            src_ref=sbuf.at[peer // nmp], dst_ref=srecv.at[owner],
            send_sem=s_ssem.at[peer], recv_sem=s_rsem.at[owner],
            device_id={"seq": peer // nmp, "mp": lax.rem(peer, nmp)}, device_id_type=MESH,
        )

    def s_start(d, carry):
        s_copy(flat, lax.rem(flat + d, total)).start()
        return carry

    def s_wait(d, carry):
        peer = lax.rem(flat + d, total)
        s_copy(peer, peer).wait_recv()
        return carry

    def s_done(d, carry):
        s_copy(flat, lax.rem(flat + d, total)).wait_send()
        return carry

    lax.fori_loop(1, total, s_start, 0)
    for peer in others_z:
        q_copy(z, peer).wait_send()
    for owner in others_z:
        for peer in others_b:
            qb_copy(owner, b, peer).wait_send()
    for c in range(chunks):
        for peer in others_x:
            out_copy(x, peer, c).wait_send()
            in_copy(x, peer, c).wait_send()
    lax.fori_loop(1, total, s_wait, 0)
    out_ref[...] = lax.fori_loop(
        1, total, lambda i, acc: acc + srecv[i].astype(jnp.float32),
        srecv[0].astype(jnp.float32),
    )
    lax.fori_loop(1, total, s_done, 0)


def per_device(
    nseq, nmp, nb,
    hidden_acts, out_cotangent, in_projection, out_projection, step_lengths, query_grads, query_trace,
):
    tokens, units = hidden_acts.shape[1:]
    features = out_cotangent.shape[2]
    rank = in_projection.shape[1]
    share = rank // nmp
    steps = step_lengths.shape[1]
    local, entries = query_grads.shape
    queries = local * nseq
    chunks = tokens // CHUNK
    mine = steps // nseq
    total = nseq * nmp
    any_spec = pl.BlockSpec(memory_space=pl.ANY)
    vmem_spec = pl.BlockSpec(memory_space=pltpu.VMEM)
    dma = pltpu.SemaphoreType.DMA
    totals = pl.pallas_call(
        functools.partial(kernel, nseq, nmp, nb),
        out_shape=jax.ShapeDtypeStruct((mine, queries), jnp.float32),
        in_specs=[any_spec, any_spec, any_spec, any_spec, vmem_spec, any_spec],
        out_specs=vmem_spec,
        scratch_shapes=[
            pltpu.VMEM((tokens, units), jnp.bfloat16),
            pltpu.VMEM((tokens, features), jnp.bfloat16),
            pltpu.VMEM((rank, units), jnp.bfloat16),
            pltpu.VMEM((rank, features), jnp.bfloat16),
            pltpu.VMEM((nseq, nb, local // nb, entries), jnp.bfloat16),
            pltpu.VMEM((chunks, nmp, rank, CHUNK), jnp.float32),
            pltpu.VMEM((chunks, nmp, share, CHUNK), jnp.float32),
            pltpu.VMEM((chunks, nmp, share, CHUNK), jnp.float32),
            pltpu.VMEM((share // GROUP * steps, GROUP * CHUNK), jnp.bfloat16),
            pltpu.VMEM((share // GROUP * steps, GROUP * rank), jnp.float32),
            pltpu.VMEM((nseq, mine, queries), jnp.bfloat16),
            pltpu.VMEM((total, mine, queries), jnp.bfloat16),
            dma((chunks,)), dma((chunks,)), dma((2,)), dma,
            dma((chunks, nmp)), dma((chunks, nmp)), dma((chunks, nmp)), dma((chunks, nmp)),
            dma((nseq,)), dma((nseq,)), dma((nseq, nb)), dma((nseq, nb)),
            dma((total,)), dma((total,)),
        ],
        compiler_params=pltpu.CompilerParams(
            collective_id=0, has_side_effects=True, vmem_limit_bytes=56 * 1024 * 1024
        ),
        cost_estimate=pl.CostEstimate(
            flops=2 * tokens * (units + features) * rank + 2 * steps * share * tokens * rank,
            bytes_accessed=2 * tokens * (units + features), transcendentals=0,
        ),
        name="influence",
    )(
        hidden_acts, out_cotangent, in_projection.T, out_projection.T, step_lengths,
        query_grads.reshape(nb, local // nb, entries),
    )
    keep = query_trace[None, :] != lax.axis_index("batch")
    return jnp.where(keep, totals, jnp.zeros((), jnp.float32))[None]


def solution(mesh):
    return jax.shard_map(
        functools.partial(per_device, mesh.shape["seq"], mesh.shape["mp"], mesh.shape["batch"]),
        mesh=mesh,
        in_specs=(
            P(("parts", "batch"), "seq", "mp"),
            P(("parts", "batch"), "seq", "mp"),
            P("mp", None),
            P("mp", None),
            P(("parts", "batch"), None),
            P("seq", "mp"),
            P(),
        ),
        out_specs=P(("parts", "batch"), "seq", None),
        check_vma=False,
    )
```

```python
import functools

import jax
import jax.numpy as jnp
from jax import lax
from jax.experimental import pallas as pl
from jax.experimental.pallas import tpu as pltpu
from jax.sharding import PartitionSpec as P

MESH = pl.DeviceIdType.MESH
CHUNK = 256
GROUP = 4
DEPTH = 2
LAG = 2


def nt(left, right):
    return lax.dot_general(
        left, right, (((1,), (1,)), ((), ())), preferred_element_type=jnp.float32
    )


def kernel(
    nseq, nmp, nb,
    hid_hbm, cot_hbm, win_hbm, wout_hbm, len_ref, q_hbm, trace_ref,
    out_ref,
    hid, cot, win, wout, qbuf, inbuf, outown, outrecv, lhs, gacc, sbuf, srecv,
    hid_sem, cot_sem, w_sem, qloc_sem,
    in_ssem, in_rsem, out_ssem, out_rsem, q_ssem, q_rsem, qb_ssem, qb_rsem, s_ssem, s_rsem,
):
    tokens = hid.shape[0]
    rank = win.shape[0]
    share = rank // nmp
    steps = len_ref.shape[1]
    chunks = tokens // CHUNK
    mine = steps // nseq
    z = lax.axis_index("seq")
    x = lax.axis_index("mp")
    b = lax.axis_index("batch")

    w_copies = [
        pltpu.make_async_copy(wout_hbm, wout, w_sem.at[0]),
        pltpu.make_async_copy(win_hbm, win, w_sem.at[1]),
    ]
    rows = lambda c: pl.ds(pl.multiple_of(c * CHUNK, CHUNK), CHUNK)

    def cot_copy(c):
        return pltpu.make_async_copy(cot_hbm.at[0, rows(c)], cot.at[rows(c)], cot_sem.at[c])

    def hid_copy(c):
        return pltpu.make_async_copy(hid_hbm.at[0, rows(c)], hid.at[rows(c)], hid_sem.at[c])

    q_local = pltpu.make_async_copy(q_hbm, qbuf.at[z], qloc_sem)
    w_copies[0].start()
    for c in range(chunks):
        cot_copy(c).start()
    w_copies[1].start()
    for c in range(min(DEPTH, chunks)):
        hid_copy(c).start()

    barrier = pltpu.get_barrier_semaphore()
    total = nseq * nmp
    flat = z * nmp + x

    def greet(d, carry):
        peer = lax.rem(flat + d, total)
        pl.semaphore_signal(
            barrier, inc=1, device_id={"seq": peer // nmp, "mp": lax.rem(peer, nmp)},
            device_id_type=MESH,
        )
        return carry

    lax.fori_loop(1, total, greet, 0)
    for d in range(1, nb):
        pl.semaphore_signal(
            barrier, inc=1, device_id={"batch": lax.rem(b + d, nb)}, device_id_type=MESH
        )
    pl.semaphore_wait(barrier, total - 1 + nb - 1)

    def q_copy(owner, peer):
        return pltpu.make_async_remote_copy(
            src_ref=q_hbm.at[b], dst_ref=qbuf.at[owner, b],
            send_sem=q_ssem.at[peer], recv_sem=q_rsem.at[owner],
            device_id={"seq": peer}, device_id_type=MESH,
        )

    def qb_copy(owner, core, peer):
        return pltpu.make_async_remote_copy(
            src_ref=qbuf.at[owner, core], dst_ref=qbuf.at[owner, core],
            send_sem=qb_ssem.at[owner, peer], recv_sem=qb_rsem.at[owner, core],
            device_id={"batch": peer}, device_id_type=MESH,
        )

    others_z = [lax.rem(z + d, nseq) for d in range(1, nseq)]
    others_x = [lax.rem(x + d, nmp) for d in range(1, nmp)]
    others_b = [lax.rem(b + d, nb) for d in range(1, nb)]
    for peer in others_z:
        q_copy(z, peer).start()

    def out_copy(owner, peer, c):
        return pltpu.make_async_remote_copy(
            src_ref=outown.at[c, peer], dst_ref=outrecv.at[c, owner],
            send_sem=out_ssem.at[c, peer], recv_sem=out_rsem.at[c, owner],
            device_id={"mp": peer}, device_id_type=MESH,
        )

    def in_copy(owner, peer, c):
        return pltpu.make_async_remote_copy(
            src_ref=inbuf.at[c, x], dst_ref=inbuf.at[c, owner],
            send_sem=in_ssem.at[c, peer], recv_sem=in_rsem.at[c, owner],
            device_id={"mp": peer}, device_id_type=MESH,
        )

    w_copies[0].wait()

    def features_step(c, carry):
        cot_copy(c).wait()
        part = nt(cot[rows(c), :], wout[...])
        outown[c] = part.T.reshape(nmp, share, CHUNK)
        for peer in others_x:
            out_copy(x, peer, c).start()
        outrecv[c, x] = outown[c, x]
        return carry

    lax.fori_loop(0, chunks, features_step, 0)

    lengths = len_ref[...].astype(jnp.float32)
    row = lax.broadcasted_iota(jnp.int32, (steps, steps), 0)
    col = lax.broadcasted_iota(jnp.int32, (steps, steps), 1)
    spread = jnp.broadcast_to(lengths, (steps, steps))
    ends = jnp.sum(jnp.where(col <= row, spread, 0.0), axis=1, keepdims=True).astype(jnp.int32)
    starts = jnp.sum(jnp.where(col < row, spread, 0.0), axis=1, keepdims=True).astype(jnp.int32)

    def project(c):
        hid_copy(c).wait()

        @pl.when(c < chunks - DEPTH)
        def _():
            hid_copy(c + DEPTH).start()

        part = nt(hid[rows(c), :], win[...])
        inbuf[c, x] = part.T
        for peer in others_x:
            in_copy(x, peer, c).start()

    def gradients(c):
        for peer in others_x:
            out_copy(peer, peer, c).wait_recv()
            in_copy(peer, peer, c).wait_recv()
        out_total = outrecv[c, 0]
        in_total = inbuf[c, 0]
        for m in range(1, nmp):
            out_total = out_total + outrecv[c, m]
            in_total = in_total + inbuf[c, m]
        out_low = out_total.astype(jnp.bfloat16).astype(jnp.float32)
        in_low = in_total.astype(jnp.bfloat16)
        pos = (
            lax.broadcasted_iota(jnp.int32, (steps, CHUNK), 1) + (z * tokens + c * CHUNK)
        )
        member = jnp.where((pos >= starts) & (pos < ends), 1.0, 0.0).astype(jnp.bfloat16)
        member = member.reshape(steps // 16, 16, CHUNK)
        zero = jnp.zeros((rank, CHUNK), jnp.bfloat16)
        right = jnp.concatenate(
            [
                jnp.concatenate([in_low if i == k else zero for i in range(GROUP)], axis=1)
                for k in range(GROUP)
            ],
            axis=0,
        )
        for j in range(share):
            line = jnp.broadcast_to(out_low[j:j + 1, :], (16, CHUNK)).astype(jnp.bfloat16)
            lhs[
                pl.ds(j // GROUP * steps, steps), pl.ds(j % GROUP * CHUNK, CHUNK)
            ] = (member * line[None]).reshape(steps, CHUNK)
        gacc[...] += nt(lhs[...], right)

    gacc[...] = jnp.zeros_like(gacc)
    w_copies[1].wait()

    def hidden_step(c, carry):
        @pl.when(c < chunks)
        def _():
            project(c)

        @pl.when(c == chunks + LAG - 1)
        def _():
            for owner in others_z:
                q_copy(owner, owner).wait_recv()
                for peer in others_b:
                    qb_copy(owner, b, peer).start()

        @pl.when(c >= LAG)
        def _():
            gradients(c - LAG)

        return carry

    q_local.start()
    lax.fori_loop(0, chunks + LAG, hidden_step, 0)

    low = jnp.concatenate(
        [gacc[pl.ds(g * steps, steps), :].astype(jnp.bfloat16) for g in range(share // GROUP)],
        axis=1,
    )
    q_local.wait()
    for owner in others_z:
        for core in others_b:
            qb_copy(owner, core, core).wait_recv()
    queries = qbuf[...].reshape(nseq * nb * qbuf.shape[2], qbuf.shape[3])
    part = nt(low, queries).astype(jnp.bfloat16)
    sbuf[...] = part.reshape(nseq, mine, part.shape[1])
    srecv[flat] = sbuf[z]

    def s_copy(owner, peer):
        return pltpu.make_async_remote_copy(
            src_ref=sbuf.at[peer // nmp], dst_ref=srecv.at[owner],
            send_sem=s_ssem.at[peer], recv_sem=s_rsem.at[owner],
            device_id={"seq": peer // nmp, "mp": lax.rem(peer, nmp)}, device_id_type=MESH,
        )

    def s_start(d, carry):
        s_copy(flat, lax.rem(flat + d, total)).start()
        return carry

    def s_wait(d, carry):
        peer = lax.rem(flat + d, total)
        s_copy(peer, peer).wait_recv()
        return carry

    def s_done(d, carry):
        s_copy(flat, lax.rem(flat + d, total)).wait_send()
        return carry

    lax.fori_loop(1, total, s_start, 0)
    for peer in others_z:
        q_copy(z, peer).wait_send()
    for owner in others_z:
        for peer in others_b:
            qb_copy(owner, b, peer).wait_send()
    for c in range(chunks):
        for peer in others_x:
            out_copy(x, peer, c).wait_send()
            in_copy(x, peer, c).wait_send()
    lax.fori_loop(1, total, s_wait, 0)
    score = lax.fori_loop(
        1, total, lambda i, acc: acc + srecv[i].astype(jnp.float32),
        srecv[0].astype(jnp.float32),
    )
    out_ref[0] = jnp.where(trace_ref[...] != b, score, 0.0)
    lax.fori_loop(1, total, s_done, 0)


def per_device(
    nseq, nmp, nb,
    hidden_acts, out_cotangent, in_projection, out_projection, step_lengths, query_grads, query_trace,
):
    tokens, units = hidden_acts.shape[1:]
    features = out_cotangent.shape[2]
    rank = in_projection.shape[1]
    share = rank // nmp
    steps = step_lengths.shape[1]
    local, entries = query_grads.shape
    queries = local * nseq
    chunks = tokens // CHUNK
    mine = steps // nseq
    total = nseq * nmp
    any_spec = pl.BlockSpec(memory_space=pl.ANY)
    vmem_spec = pl.BlockSpec(memory_space=pltpu.VMEM)
    dma = pltpu.SemaphoreType.DMA
    return pl.pallas_call(
        functools.partial(kernel, nseq, nmp, nb),
        out_shape=jax.ShapeDtypeStruct((1, mine, queries), jnp.float32),
        in_specs=[any_spec, any_spec, any_spec, any_spec, vmem_spec, any_spec, vmem_spec],
        out_specs=vmem_spec,
        scratch_shapes=[
            pltpu.VMEM((tokens, units), jnp.bfloat16),
            pltpu.VMEM((tokens, features), jnp.bfloat16),
            pltpu.VMEM((rank, units), jnp.bfloat16),
            pltpu.VMEM((rank, features), jnp.bfloat16),
            pltpu.VMEM((nseq, nb, local // nb, entries), jnp.bfloat16),
            pltpu.VMEM((chunks, nmp, rank, CHUNK), jnp.float32),
            pltpu.VMEM((chunks, nmp, share, CHUNK), jnp.float32),
            pltpu.VMEM((chunks, nmp, share, CHUNK), jnp.float32),
            pltpu.VMEM((share // GROUP * steps, GROUP * CHUNK), jnp.bfloat16),
            pltpu.VMEM((share // GROUP * steps, GROUP * rank), jnp.float32),
            pltpu.VMEM((nseq, mine, queries), jnp.bfloat16),
            pltpu.VMEM((total, mine, queries), jnp.bfloat16),
            dma((chunks,)), dma((chunks,)), dma((2,)), dma,
            dma((chunks, nmp)), dma((chunks, nmp)), dma((chunks, nmp)), dma((chunks, nmp)),
            dma((nseq,)), dma((nseq,)), dma((nseq, nb)), dma((nseq, nb)),
            dma((total,)), dma((total,)),
        ],
        compiler_params=pltpu.CompilerParams(
            collective_id=0, has_side_effects=True, vmem_limit_bytes=56 * 1024 * 1024
        ),
        cost_estimate=pl.CostEstimate(
            flops=2 * tokens * (units + features) * rank + 2 * steps * share * tokens * rank,
            bytes_accessed=2 * tokens * (units + features), transcendentals=0,
        ),
        name="influence",
    )(
        hidden_acts, out_cotangent, in_projection.T, out_projection.T, step_lengths,
        query_grads.reshape(nb, local // nb, entries), query_trace[None],
    )


def solution(mesh):
    return jax.shard_map(
        functools.partial(per_device, mesh.shape["seq"], mesh.shape["mp"], mesh.shape["batch"]),
        mesh=mesh,
        in_specs=(
            P(("parts", "batch"), "seq", "mp"),
            P(("parts", "batch"), "seq", "mp"),
            P("mp", None),
            P("mp", None),
            P(("parts", "batch"), None),
            P("seq", "mp"),
            P(),
        ),
        out_specs=P(("parts", "batch"), "seq", None),
        check_vma=False,
    )
```
